768 devices in a mesh: dp: 64 (over x, y, core), seq: 12 (over z).
Axes of the slice: x: 4, y: 8, z: 12, core: 2. Of those that a mesh axis runs over, the one named last changes fastest.
Arguments:
- token_ids: int32 [98304], P('dp'), may hold values from 0 to 127999, as said below
- embed_table: bfloat16 [128000, 2304], P('dp', 'seq'), may hold values from -0.125 to 0.125
- second_moment: bfloat16 [128000, 2304], P('dp', 'seq'), may hold values from 0.099609375 to 4
- cotangent: bfloat16 [98304, 2304], P(('dp', 'seq')), may hold values from -0.125 to 0.125
Outputs:
- embedded: bfloat16 [98304, 2304], P(('dp', 'seq'))
- new_table: bfloat16 [128000, 2304], P('dp', 'seq')
- new_moment: bfloat16 [128000, 2304], P('dp', 'seq')
The draws below stay inside these ranges and needn't reach their ends.
Inputs may be any that keep to these rules, and one draw needn't show every extreme that they name: `token_ids`: among the tokens of one index of dp at most 16 distinct ids lie in one block of 2000 consecutive ids; in every draw some block holds exactly 16 distinct ids of every index's tokens.
All inputs are finite; a program needn't handle non-finite values.
Results may differ from the reference program's by a relative error of at most 0.008.
Values may be sent and summed in bfloat16 or wider, within the bound.
No kernel may reach another device: no remote copies, remote signals or barrier semaphores. Data moves between devices by JAX's collectives and lax.ppermute only.
A program may use at most 64 MiB of HBM per device.

```python
import math
import jax
import jax.numpy as jnp

D = 2304
VROWS = 2000
CAP = 16
STEP = 1000
VOCAB = 128000
TOKENS = 98304


def draw_token_ids(key, part):
    key = jax.random.fold_in(key, 11)
    owner_count = VOCAB // VROWS
    group_size = TOKENS // owner_count
    count_key, hot_key, pick_key = jax.random.split(key, 3)
    row_counts = jax.random.randint(count_key, (owner_count, owner_count), 1, CAP + 1)
    hot_owner = jax.random.randint(hot_key, (), 0, owner_count)
    row_counts = jnp.where(jnp.arange(owner_count, dtype=jnp.int32)[None, :] == hot_owner, CAP, row_counts)
    group_keys = jax.random.split(pick_key, owner_count)

    def one_group(group_key, counts_row):
        draw_keys = jax.random.split(group_key, 5)
        scores = jax.random.randint(draw_keys[4], (owner_count, VROWS), 0, 2 ** 30 // VROWS) * VROWS
        scores = scores + jnp.arange(VROWS, dtype=jnp.int32)[None, :]
        ranking = jnp.argsort(scores, axis=1)[:, :CAP].astype(jnp.int32)
        id_table = (jnp.arange(owner_count, dtype=jnp.int32)[None, :] * VROWS + ranking.T).reshape(-1)
        live = (jnp.arange(CAP, dtype=jnp.int32)[:, None] < counts_row[None, :]).reshape(-1)
        live_count = jnp.sum(live.astype(jnp.int32))
        placed = jnp.argsort(1 - live.astype(jnp.int32), stable=True)
        entries = id_table[placed]
        first_u = jax.random.randint(draw_keys[0], (group_size,), 0, 1024)
        second_u = jax.random.randint(draw_keys[1], (group_size,), 0, 1024)
        third_u = jax.random.randint(draw_keys[2], (group_size,), 0, 1024)
        skewed = first_u * second_u // 1024 * third_u // 1024
        position = jnp.arange(group_size, dtype=jnp.int32)
        chosen = jnp.where(position < live_count, position, skewed * live_count // 1024)
        return jax.random.permutation(draw_keys[3], entries[chosen])
    return jax.vmap(one_group)(group_keys, row_counts).reshape(-1).astype(jnp.int32)


def shard_levels(own_key, shape, shards, low, high):
    gain = 1.0
    for dim, shards_of in shards:
        draws = jax.random.uniform(jax.random.fold_in(jax.random.fold_in(own_key, 6), dim), (shards_of,), jnp.float32, low / len(shards), high / len(shards))
        gain = gain * jnp.repeat(jnp.exp(draws), shape[dim] // shards_of).reshape((-1,) + (1,) * (len(shape) - 1 - dim))
    return gain


def scatter_about(key, shape, deviation, reach, cuts=(), held_as=jnp.bfloat16):
    drawn = deviation * jax.random.normal(key, shape, jnp.float32)
    if cuts:
        drawn = drawn * shard_levels(key, shape, cuts, -0.22, 0.18)
    return jnp.clip(drawn, -reach, reach).astype(held_as)


def setup_inputs(seed: int = 0) -> dict:
    keys = jax.random.split(jax.random.key(seed), 5)
    token_ids = draw_token_ids(jax.random.fold_in(keys[4], 71), 0)
    embed_table = scatter_about(keys[1], (VOCAB, D), D ** -0.5, 0.125, ((0, 64), (1, 12)))
    second_moment = jnp.clip(jnp.exp(math.log(4.0) - 3.6927934 * jax.random.uniform(keys[2], (VOCAB, D), jnp.float32) ** shard_levels(keys[2], (VOCAB, D), ((0, 64), (1, 12)), -0.2, 0.2)), 0.099609375, 4.0).astype(jnp.bfloat16)
    cotangent = scatter_about(keys[3], (TOKENS, D), 0.02, 0.125, ((0, 768),))
    return dict(token_ids=token_ids, embed_table=embed_table, second_moment=second_moment, cotangent=cotangent)


beta_two = 0.95
epsilon = 1e-08
learn_rate = 0.01
weight_decay = 0.1

def reference(token_ids, embed_table, second_moment, cotangent):
    normalizer = math.sqrt(D)
    fetched = jnp.take(embed_table, token_ids, axis=0).astype(jnp.float32)
    embedded = (fetched * normalizer).astype(jnp.bfloat16)
    summed = jax.ops.segment_sum(cotangent.astype(jnp.float32), token_ids, num_segments=VOCAB)
    hit_count = jax.ops.segment_sum(jnp.ones_like(token_ids), token_ids, num_segments=VOCAB)
    touched = (hit_count > 0)[:, None]
    gradient = summed * normalizer
    weights = embed_table.astype(jnp.float32)
    moment_new = beta_two * second_moment.astype(jnp.float32) + (1.0 - beta_two) * gradient * gradient
    denominator = jnp.sqrt(moment_new / (1.0 - beta_two ** STEP)) + epsilon
    updated = weights - learn_rate * (gradient / denominator + weight_decay * weights)
    new_table = jnp.where(touched, updated.astype(jnp.bfloat16), embed_table)
    new_moment = jnp.where(touched, moment_new.astype(jnp.bfloat16), second_moment)
    return (embedded, new_table, new_moment)
```

```python
import functools
import math

import jax
import jax.numpy as jnp
from jax import lax
from jax.experimental import pallas as pl
from jax.experimental.pallas import tpu as pltpu
from jax.sharding import PartitionSpec as P

D = 2304
CAP = 16
STEP = 1000
VOCAB_ROWS = 2000

beta_two = 0.95
epsilon = 1e-08
learn_rate = 0.01
weight_decay = 0.1

BF16 = jnp.bfloat16
F32 = jnp.float32
I32 = jnp.int32
VMEM_LIMIT = 48 * 1024 * 1024


def call(kernel, out_shape, n_in, scratch=(), smem_in=(), flops=0, nbytes=0):
    def spec(i):
        return pl.BlockSpec(memory_space=pltpu.SMEM if i in smem_in else pltpu.VMEM)

    many = isinstance(out_shape, (list, tuple))
    return pl.pallas_call(
        kernel,
        out_shape=out_shape,
        in_specs=[spec(i) for i in range(n_in)],
        out_specs=[pl.BlockSpec(memory_space=pltpu.VMEM) for _ in out_shape]
        if many
        else pl.BlockSpec(memory_space=pltpu.VMEM),
        scratch_shapes=list(scratch),
        compiler_params=pltpu.CompilerParams(vmem_limit_bytes=VMEM_LIMIT),
        cost_estimate=pl.CostEstimate(flops=flops, bytes_accessed=nbytes, transcendentals=0),
    )


def iota(shape, dim):
    return lax.broadcasted_iota(I32, shape, dim)


def pack_cotangent(cot_ref, out_ref):
    for peer in range(out_ref.shape[0]):
        block = cot_ref[:, 192 * peer : 192 * peer + 192]
        out_ref[peer, 0:128, :] = block[:, 0:128]
        out_ref[peer, 128:192, :] = jnp.concatenate(
            [block[0:64, 128:192], block[64:128, 128:192]], axis=1
        )


def unpack_tokens(in_ref, out_ref):
    for peer in range(in_ref.shape[0]):
        tail = in_ref[peer, 128:192, :]
        out_ref[:, 192 * peer : 192 * peer + 128] = in_ref[peer, 0:128, :]
        out_ref[:, 192 * peer + 128 : 192 * peer + 192] = jnp.concatenate(
            [tail[:, 0:64], tail[:, 64:128]], axis=0
        )


def columns_of(row):
    return jnp.transpose(jnp.broadcast_to(row, (128, 128)))


def number_slots(me_ref, ids_ref, slot_ref, want_ref, id_cols, first_cols, first_rows):
    blocks = ids_ref.shape[0]
    me = me_ref[0]
    ids = ids_ref[...].astype(F32)
    for i in range(blocks):
        id_cols[i] = columns_of(ids[i : i + 1, :])
    earlier = iota((128, 128), 0) < iota((128, 128), 1)
    for j in range(blocks):
        row = ids[j : j + 1, :]
        seen = jnp.where((id_cols[j] == row) & earlier, 1.0, 0.0)
        for i in range(j):
            seen = jnp.where(id_cols[i] == row, 1.0, seen)
        again = jnp.max(seen, axis=0, keepdims=True) > 0.0
        firsts = jnp.where(again, -1.0, row)
        first_rows[j : j + 1, :] = firsts
        first_cols[j] = columns_of(firsts)
    owner = jnp.floor((ids + 0.5) * (1.0 / VOCAB_ROWS))
    base = owner * float(VOCAB_ROWS)
    local_row = ids - base
    total_hi = jnp.zeros((8, 128), F32)
    total_lo = jnp.zeros((8, 128), F32)
    for j in range(blocks):
        row = ids[j : j + 1, :]
        low = base[j : j + 1, :]
        count = jnp.zeros((128, 128), F32)
        for i in range(blocks):
            other = first_cols[i]
            count = jnp.where((other >= low) & (other < row), count + 1.0, count)
        rank = jnp.sum(count, axis=0, keepdims=True).astype(I32)
        owner_j = owner[j : j + 1, :].astype(I32)
        slot_ref[j : j + 1, :] = owner_j * CAP + rank
        relative = (owner_j ^ me) * CAP + rank
        is_first = first_rows[j : j + 1, :] >= 0.0
        local_j = local_row[j : j + 1, :].astype(I32)
        high = jnp.where(is_first, local_j >> 4, 0).astype(F32)
        lows = jnp.where(is_first, (local_j & 15) + 1, 0).astype(F32)
        left = jnp.where((relative >> 7) == iota((8, 128), 0), 1.0, 0.0).astype(BF16)
        here = (relative & 127) == iota((128, 128), 0)
        nt = (((1,), (1,)), ((), ()))
        total_hi += lax.dot_general(
            left, jnp.where(here, high, 0.0).astype(BF16), nt, preferred_element_type=F32
        )
        total_lo += lax.dot_general(
            left, jnp.where(here, lows, 0.0).astype(BF16), nt, preferred_element_type=F32
        )
    want_ref[...] = (total_hi * 16.0 + total_lo).astype(I32) - 1


def wanted_rows(me, want):
    pieces = []
    slots = 8 * 128
    position = iota((slots, 128), 0) ^ (me * CAP)
    want_f = want.astype(F32)
    spread = jnp.zeros((slots, 128), F32)
    for r in range(8):
        spread = jnp.where((position >> 7) == r, want_f[r : r + 1, :], spread)
    mine = jnp.where((position & 127) == iota((slots, 128), 1), spread, 0.0)
    del pieces
    return jnp.sum(mine, axis=1, keepdims=True).astype(I32)


def fetch_rows(me_ref, want_ref, table_ref, rows_ref):
    wanted = wanted_rows(me_ref[0], want_ref[...])
    slots, owned = wanted.shape[0], table_ref.shape[1]
    pick = jnp.where(wanted == iota((slots, owned), 1), 1.0, 0.0).astype(BF16)
    rows_ref[...] = lax.dot_general(
        pick, table_ref[...], (((1,), (1,)), ((), ())), preferred_element_type=F32
    ).astype(BF16)


def sum_slots(cols_ref, slot_ref, rows_ref, out_ref, columns):
    blocks = cols_ref.shape[0]
    slots = rows_ref.shape[0]
    for u in range(blocks):
        tail = cols_ref[u, 128:192, :]
        columns[128 * u : 128 * u + 128, 0:128] = cols_ref[u, 0:128, :]
        columns[128 * u : 128 * u + 128, 128:192] = jnp.concatenate(
            [tail[:, 0:64], tail[:, 64:128]], axis=0
        )
    member = jnp.concatenate(
        [
            jnp.where(slot_ref[u : u + 1, :] == iota((slots, 128), 0), 1.0, 0.0).astype(BF16)
            for u in range(blocks)
        ],
        axis=1,
    )
    grads = jnp.dot(member, columns[...], preferred_element_type=F32).astype(BF16)
    owners = slots // CAP
    rows = rows_ref[...]
    out_ref[:, 0:16, :] = rows[:, 0:128].reshape(owners, CAP, 128)
    out_ref[:, 16:32, :] = grads[:, 0:128].reshape(owners, CAP, 128)
    out_ref[:, 32:48, :] = jnp.concatenate([rows[:, 128:192], grads[:, 128:192]], axis=1).reshape(
        owners, CAP, 128
    )


def spread_tokens(got_ref, slot_ref, out_ref):
    blocks = slot_ref.shape[0]
    owners = got_ref.shape[0]
    slots = owners * CAP
    normalizer = math.sqrt(D)
    main = got_ref[:, 0:16, :].reshape(slots, 128)
    tail = got_ref[:, 32:48, :].reshape(slots, 128)[:, 0:64]
    rows = jnp.concatenate([main, tail], axis=1)
    slot_f = slot_ref[...].astype(F32)
    for u in range(blocks):
        mine = columns_of(slot_f[u : u + 1, :])
        pick = jnp.concatenate(
            [
                jnp.where(mine == (iota((128, 128), 1) + 128 * k).astype(F32), 1.0, 0.0).astype(BF16)
                for k in range(slots // 128)
            ],
            axis=1,
        )
        tokens = (jnp.dot(pick, rows, preferred_element_type=F32) * normalizer).astype(BF16)
        out_ref[u, 0:128, :] = tokens[:, 0:128]
        out_ref[u, 128:192, :] = jnp.concatenate(
            [tokens[0:64, 128:192], tokens[64:128, 128:192]], axis=1
        )


def update_rows(me_ref, want_ref, got_ref, table_ref, moment_ref, new_table_ref, new_moment_ref):
    normalizer = math.sqrt(D)
    wanted = wanted_rows(me_ref[0], want_ref[...])
    slots, owned = wanted.shape[0], table_ref.shape[1]
    pick = jnp.where(wanted == iota((slots, owned), 1), 1.0, 0.0).astype(BF16)
    main = got_ref[:, 16:32, :].reshape(slots, 128)
    tail = got_ref[:, 32:48, :].reshape(slots, 128)
    tn = (((0,), (0,)), ((), ()))
    ones = jnp.ones((8, slots), BF16)
    hits = jnp.dot(ones, pick, preferred_element_type=F32)
    touched = hits[0:1, :] > 0.0
    sum_main = lax.dot_general(main, pick, tn, preferred_element_type=F32)
    sum_tail = lax.dot_general(tail, pick, tn, preferred_element_type=F32)[64:128, :]
    for lo, hi, summed in ((0, 128, sum_main), (128, 192, sum_tail)):
        gradient = summed * normalizer
        old_table = table_ref[lo:hi, :]
        old_moment = moment_ref[lo:hi, :]
        weights = old_table.astype(F32)
        moment_new = beta_two * old_moment.astype(F32) + (1.0 - beta_two) * gradient * gradient
        denominator = jnp.sqrt(moment_new / (1.0 - beta_two**STEP)) + epsilon
        updated = weights - learn_rate * (gradient / denominator + weight_decay * weights)
        new_table_ref[lo:hi, :] = jnp.where(touched, updated, weights).astype(BF16)
        new_moment_ref[lo:hi, :] = jnp.where(
            touched, moment_new, old_moment.astype(F32)
        ).astype(BF16)


def exchange_requests(want, dp_count):
    position = iota((8, 128), 0) * 8 + iota((8, 128), 1) // CAP
    bit = 1
    while bit < dp_count:
        pairs = [(g, g ^ bit) for g in range(dp_count)]
        got = lax.ppermute(want, "dp", pairs)
        want = jnp.where((position & bit) != 0, got, want)
        bit *= 2
    return want


def local(token_ids, embed_table, second_moment, cotangent):
    dp_count = lax.axis_size("dp")
    seq_count = lax.axis_size("seq")
    blocks = token_ids.shape[0] // 128
    slots = dp_count * CAP
    owned = embed_table.shape[0]
    S = jax.ShapeDtypeStruct
    me = lax.axis_index("dp").astype(I32).reshape(1)
    table = embed_table.T
    moment = second_moment.T
    ids = token_ids.reshape(blocks, 128)

    packed = call(pack_cotangent, S((seq_count, 192, 128), BF16), 1, nbytes=1200000)(cotangent)
    columns = lax.all_to_all(packed, "seq", split_axis=0, concat_axis=0, tiled=True)
    slot, want = call(
        number_slots,
        (S((blocks, 128), I32), S((8, 128), I32)),
        2,
        scratch=[
            pltpu.VMEM((blocks, 128, 128), F32),
            pltpu.VMEM((blocks, 128, 128), F32),
            pltpu.VMEM((16, 128), F32),
        ],
        smem_in=(0,),
        flops=10**6,
        nbytes=10**6,
    )(me, ids)
    want = exchange_requests(want, dp_count)
    rows = call(
        fetch_rows, S((slots, 192), BF16), 3, smem_in=(0,), flops=2 * slots * owned * 192, nbytes=1200000
    )(me, want, table)
    payload = call(
        sum_slots,
        S((dp_count, 48, 128), BF16),
        3,
        scratch=[pltpu.VMEM((blocks * 128, 192), BF16)],
        flops=2 * slots * blocks * 128 * 192,
        nbytes=1800000,
    )(columns, slot, rows)
    got = lax.all_to_all(payload, "dp", split_axis=0, concat_axis=0, tiled=True)
    tokens = call(
        spread_tokens, S((seq_count, 192, 128), BF16), 2, flops=2 * slots * blocks * 128 * 192, nbytes=1400000
    )(got, slot)
    arrived = lax.all_to_all(tokens, "seq", split_axis=0, concat_axis=0, tiled=True)
    new_table, new_moment = call(
        update_rows,
        (S((192, owned), BF16), S((192, owned), BF16)),
        5,
        smem_in=(0,),
        flops=2 * slots * owned * 192,
        nbytes=4000000,
    )(me, want, got, table, moment)
    embedded = call(unpack_tokens, S((128, seq_count * 192), BF16), 1, nbytes=1200000)(arrived)
    return embedded, new_table.T, new_moment.T


def solution(mesh):
    in_specs = (P("dp"), P("dp", "seq"), P("dp", "seq"), P(("dp", "seq"), None))
    out_specs = (P(("dp", "seq"), None), P("dp", "seq"), P("dp", "seq"))
    return jax.shard_map(local, mesh=mesh, in_specs=in_specs, out_specs=out_specs, check_vma=False)
```

```python
import functools
import math

import jax
import jax.numpy as jnp
from jax import lax
from jax.experimental import pallas as pl
from jax.experimental.pallas import tpu as pltpu
from jax.sharding import PartitionSpec as P

D = 2304
CAP = 16
STEP = 1000
VOCAB_ROWS = 2000

beta_two = 0.95
epsilon = 1e-08
learn_rate = 0.01
weight_decay = 0.1

GRADS_ORDER = [(1 * k + 11) % 12 for k in range(12)]
ROWS_ORDER = [(1 * k + 5) % 12 for k in range(12)]

FLIP = 8

BF16 = jnp.bfloat16
F32 = jnp.float32
I32 = jnp.int32
VMEM_LIMIT = 48 * 1024 * 1024


def call(kernel, out_shape, n_in, scratch=(), smem_in=(), flops=0, nbytes=0):
    def spec(i):
        return pl.BlockSpec(memory_space=pltpu.SMEM if i in smem_in else pltpu.VMEM)

    many = isinstance(out_shape, (list, tuple))
    return pl.pallas_call(
        kernel,
        out_shape=out_shape,
        in_specs=[spec(i) for i in range(n_in)],
        out_specs=[pl.BlockSpec(memory_space=pltpu.VMEM) for _ in out_shape]
        if many
        else pl.BlockSpec(memory_space=pltpu.VMEM),
        scratch_shapes=list(scratch),
        compiler_params=pltpu.CompilerParams(vmem_limit_bytes=VMEM_LIMIT),
        cost_estimate=pl.CostEstimate(flops=flops, bytes_accessed=nbytes, transcendentals=0),
    )


def iota(shape, dim):
    return lax.broadcasted_iota(I32, shape, dim)


def pack_cotangent(cot_ref, out_ref):
    for peer in range(out_ref.shape[0]):
        block = cot_ref[:, 192 * peer : 192 * peer + 192]
        place = GRADS_ORDER.index(peer)
        out_ref[place, 0:128, :] = block[:, 0:128]
        out_ref[place, 128:192, :] = jnp.concatenate(
            [block[0:64, 128:192], block[64:128, 128:192]], axis=1
        )


def unpack_tokens(in_ref, out_ref):
    for peer in range(in_ref.shape[0]):
        place = ROWS_ORDER.index(peer)
        tail = in_ref[place, 128:192, :]
        out_ref[:, 192 * peer : 192 * peer + 128] = in_ref[place, 0:128, :]
        out_ref[:, 192 * peer + 128 : 192 * peer + 192] = jnp.concatenate(
            [tail[:, 0:64], tail[:, 64:128]], axis=0
        )


def columns_of(row):
    return jnp.transpose(jnp.broadcast_to(row, (128, 128)))


def number_slots(me_ref, ids_ref, slot_ref, want_ref, id_cols, first_cols, first_rows):
    blocks = ids_ref.shape[0]
    me = me_ref[0] & 15
    ids = ids_ref[...].astype(F32)
    for i in range(blocks):
        id_cols[i] = columns_of(ids[i : i + 1, :])
    earlier = iota((128, 128), 0) < iota((128, 128), 1)
    for j in range(blocks):
        row = ids[j : j + 1, :]
        seen = jnp.where((id_cols[j] == row) & earlier, 1.0, 0.0)
        for i in range(j):
            seen = jnp.where(id_cols[i] == row, 1.0, seen)
        again = jnp.max(seen, axis=0, keepdims=True) > 0.0
        firsts = jnp.where(again, -1.0, row)
        first_rows[j : j + 1, :] = firsts
        first_cols[j] = columns_of(firsts)
    owner = jnp.floor((ids + 0.5) * (1.0 / VOCAB_ROWS))
    base = owner * float(VOCAB_ROWS)
    local_row = ids - base
    total_hi = jnp.zeros((8, 128), F32)
    total_lo = jnp.zeros((8, 128), F32)
    for j in range(blocks):
        row = ids[j : j + 1, :]
        low = base[j : j + 1, :]
        count = jnp.zeros((128, 128), F32)
        for i in range(blocks):
            other = first_cols[i]
            count = jnp.where((other >= low) & (other < row), count + 1.0, count)
        rank = jnp.sum(count, axis=0, keepdims=True).astype(I32)
        owner_j = owner[j : j + 1, :].astype(I32)
        slot_ref[j : j + 1, :] = (owner_j ^ FLIP) * CAP + rank
        relative = (owner_j ^ me) * CAP + rank
        is_first = first_rows[j : j + 1, :] >= 0.0
        local_j = local_row[j : j + 1, :].astype(I32)
        high = jnp.where(is_first, local_j >> 4, 0).astype(F32)
        lows = jnp.where(is_first, (local_j & 15) + 1, 0).astype(F32)
        left = jnp.where((relative >> 7) == iota((8, 128), 0), 1.0, 0.0).astype(BF16)
        here = (relative & 127) == iota((128, 128), 0)
        nt = (((1,), (1,)), ((), ()))
        total_hi += lax.dot_general(
            left, jnp.where(here, high, 0.0).astype(BF16), nt, preferred_element_type=F32
        )
        total_lo += lax.dot_general(
            left, jnp.where(here, lows, 0.0).astype(BF16), nt, preferred_element_type=F32
        )
    want = (total_hi * 16.0 + total_lo).astype(I32) - 1
    for x in range(4):
        want_ref[x] = want[2 * x : 2 * x + 2, :]


def wanted_rows(me, want):
    slots = 8 * 128
    position = iota((slots, 128), 0) ^ (((me & 15) ^ FLIP) * CAP)
    want_f = want.astype(F32)
    spread = jnp.zeros((slots, 128), F32)
    for r in range(8):
        spread = jnp.where((position >> 7) == r, want_f[r // 2, r % 2 : r % 2 + 1, :], spread)
    mine = jnp.where((position & 127) == iota((slots, 128), 1), spread, 0.0)
    return jnp.sum(mine, axis=1, keepdims=True).astype(I32)


def fetch_rows(me_ref, want_ref, table_ref, rows_ref):
    wanted = wanted_rows(me_ref[0], want_ref[...])
    slots, owned = wanted.shape[0], table_ref.shape[1]
    pick = jnp.where(wanted == iota((slots, owned), 1), 1.0, 0.0).astype(BF16)
    rows_ref[...] = lax.dot_general(
        pick, table_ref[...], (((1,), (1,)), ((), ())), preferred_element_type=F32
    ).astype(BF16)


def sum_slots(cols_ref, slot_ref, rows_ref, out_ref, columns):
    blocks = cols_ref.shape[0]
    slots = rows_ref.shape[0]
    for u in range(blocks):
        place = GRADS_ORDER.index(u)
        tail = cols_ref[place, 128:192, :]
        columns[128 * u : 128 * u + 128, 0:128] = cols_ref[place, 0:128, :]
        columns[128 * u : 128 * u + 128, 128:192] = jnp.concatenate(
            [tail[:, 0:64], tail[:, 64:128]], axis=0
        )
    member = jnp.concatenate(
        [
            jnp.where(slot_ref[u : u + 1, :] == iota((slots, 128), 0), 1.0, 0.0).astype(BF16)
            for u in range(blocks)
        ],
        axis=1,
    )
    grads = jnp.dot(member, columns[...], preferred_element_type=F32).astype(BF16)
    owners = slots // CAP
    rows = rows_ref[...]
    out_ref[:, 0:16, :] = rows[:, 0:128].reshape(owners, CAP, 128)
    out_ref[:, 16:32, :] = grads[:, 0:128].reshape(owners, CAP, 128)
    out_ref[:, 32:48, :] = jnp.concatenate([rows[:, 128:192], grads[:, 128:192]], axis=1).reshape(
        owners, CAP, 128
    )


def spread_tokens(got_ref, slot_ref, out_ref):
    blocks = slot_ref.shape[0]
    owners = got_ref.shape[0]
    slots = owners * CAP
    normalizer = math.sqrt(D)
    main = got_ref[:, 0:16, :].reshape(slots, 128)
    tail = got_ref[:, 32:48, :].reshape(slots, 128)[:, 0:64]
    rows = jnp.concatenate([main, tail], axis=1)
    slot_f = slot_ref[...].astype(F32)
    for u in range(blocks):
        mine = columns_of(slot_f[u : u + 1, :])
        pick = jnp.concatenate(
            [
                jnp.where(mine == (iota((128, 128), 1) + 128 * k).astype(F32), 1.0, 0.0).astype(BF16)
                for k in range(slots // 128)
            ],
            axis=1,
        )
        tokens = (jnp.dot(pick, rows, preferred_element_type=F32) * normalizer).astype(BF16)
        place = ROWS_ORDER.index(u)
        out_ref[place, 0:128, :] = tokens[:, 0:128]
        out_ref[place, 128:192, :] = jnp.concatenate(
            [tokens[0:64, 128:192], tokens[64:128, 128:192]], axis=1
        )


def update_rows(me_ref, want_ref, got_ref, table_ref, moment_ref, new_table_ref, new_moment_ref):
    normalizer = math.sqrt(D)
    wanted = wanted_rows(me_ref[0], want_ref[...])
    slots, owned = wanted.shape[0], table_ref.shape[1]
    pick = jnp.where(wanted == iota((slots, owned), 1), 1.0, 0.0).astype(BF16)
    main = got_ref[:, 16:32, :].reshape(slots, 128)
    tail = got_ref[:, 32:48, :].reshape(slots, 128)
    tn = (((0,), (0,)), ((), ()))
    ones = jnp.ones((8, slots), BF16)
    hits = jnp.dot(ones, pick, preferred_element_type=F32)
    touched = hits[0:1, :] > 0.0
    sum_main = lax.dot_general(main, pick, tn, preferred_element_type=F32)
    sum_tail = lax.dot_general(tail, pick, tn, preferred_element_type=F32)[64:128, :]
    for lo, hi, summed in ((0, 128, sum_main), (128, 192, sum_tail)):
        gradient = summed * normalizer
        old_table = table_ref[lo:hi, :]
        old_moment = moment_ref[lo:hi, :]
        weights = old_table.astype(F32)
        moment_new = beta_two * old_moment.astype(F32) + (1.0 - beta_two) * gradient * gradient
        denominator = jnp.sqrt(moment_new / (1.0 - beta_two**STEP)) + epsilon
        updated = weights - learn_rate * (gradient / denominator + weight_decay * weights)
        new_table_ref[lo:hi, :] = jnp.where(touched, updated, weights).astype(BF16)
        new_moment_ref[lo:hi, :] = jnp.where(
            touched, moment_new, old_moment.astype(F32)
        ).astype(BF16)


def exchange_requests(want, dp_count):
    across_x = [[x * 16 + rest for x in range(4)] for rest in range(16)]
    want = lax.all_to_all(
        want, "dp", split_axis=0, concat_axis=0, tiled=True, axis_index_groups=across_x
    )
    position = iota(want.shape, 1) * 8 + iota(want.shape, 2) // CAP
    for bit in (1, 2, 4, 8):
        got = lax.ppermute(want, "dp", [(g, g ^ bit) for g in range(dp_count)])
        want = jnp.where((position & bit) != 0, got, want)
    return want


def local(token_ids, embed_table, second_moment, cotangent):
    dp_count = lax.axis_size("dp")
    seq_count = lax.axis_size("seq")
    blocks = token_ids.shape[0] // 128
    slots = dp_count * CAP
    owned = embed_table.shape[0]
    S = jax.ShapeDtypeStruct
    me = lax.axis_index("dp").astype(I32).reshape(1)
    table = embed_table.T
    moment = second_moment.T
    ids = token_ids.reshape(blocks, 128)

    packed = call(pack_cotangent, S((seq_count, 192, 128), BF16), 1, nbytes=1200000)(cotangent)
    columns = lax.all_to_all(
        packed, "seq", split_axis=0, concat_axis=0, tiled=True, axis_index_groups=[GRADS_ORDER]
    )
    slot, want = call(
        number_slots,
        (S((blocks, 128), I32), S((4, 2, 128), I32)),
        2,
        scratch=[
            pltpu.VMEM((blocks, 128, 128), F32),
            pltpu.VMEM((blocks, 128, 128), F32),
            pltpu.VMEM((16, 128), F32),
        ],
        smem_in=(0,),
        flops=10**6,
        nbytes=10**6,
    )(me, ids)
    want = exchange_requests(want, dp_count)
    rows = call(
        fetch_rows, S((slots, 192), BF16), 3, smem_in=(0,), flops=2 * slots * owned * 192, nbytes=1200000
    )(me, want, table)
    payload = call(
        sum_slots,
        S((dp_count, 48, 128), BF16),
        3,
        scratch=[pltpu.VMEM((blocks * 128, 192), BF16)],
        flops=2 * slots * blocks * 128 * 192,
        nbytes=1800000,
    )(columns, slot, rows)
    flipped = [[k ^ FLIP for k in range(dp_count)]]
    got = lax.all_to_all(
        payload, "dp", split_axis=0, concat_axis=0, tiled=True, axis_index_groups=flipped
    )
    tokens = call(
        spread_tokens, S((seq_count, 192, 128), BF16), 2, flops=2 * slots * blocks * 128 * 192, nbytes=1400000
    )(got, slot)
    arrived = lax.all_to_all(
        tokens, "seq", split_axis=0, concat_axis=0, tiled=True, axis_index_groups=[ROWS_ORDER]
    )
    new_table, new_moment = call(
        update_rows,
        (S((192, owned), BF16), S((192, owned), BF16)),
        5,
        smem_in=(0,),
        flops=2 * slots * owned * 192,
        nbytes=4000000,
    )(me, want, got, table, moment)
    embedded = call(unpack_tokens, S((128, seq_count * 192), BF16), 1, nbytes=1200000)(arrived)
    return embedded, new_table.T, new_moment.T


def solution(mesh):
    in_specs = (P("dp"), P("dp", "seq"), P("dp", "seq"), P(("dp", "seq"), None))
    out_specs = (P(("dp", "seq"), None), P("dp", "seq"), P("dp", "seq"))
    return jax.shard_map(local, mesh=mesh, in_specs=in_specs, out_specs=out_specs, check_vma=False)
```

```python
import functools
import math

import jax
import jax.numpy as jnp
from jax import lax
from jax.experimental import pallas as pl
from jax.experimental.pallas import tpu as pltpu
from jax.sharding import PartitionSpec as P

D = 2304
CAP = 16
STEP = 1000
VOCAB_ROWS = 2000

beta_two = 0.95
epsilon = 1e-08
learn_rate = 0.01
weight_decay = 0.1

GRADS_ORDER = [(1 * k + 11) % 12 for k in range(12)]
ROWS_ORDER = [(1 * k + 5) % 12 for k in range(12)]

FLIP = 8

BF16 = jnp.bfloat16
F32 = jnp.float32
I32 = jnp.int32
VMEM_LIMIT = 48 * 1024 * 1024


def call(kernel, out_shape, n_in, scratch=(), smem_in=(), out_space=pltpu.VMEM, flops=0, nbytes=0):
    def spec(i):
        return pl.BlockSpec(memory_space=pltpu.SMEM if i in smem_in else pltpu.VMEM)

    many = isinstance(out_shape, (list, tuple))
    return pl.pallas_call(
        kernel,
        out_shape=out_shape,
        in_specs=[spec(i) for i in range(n_in)],
        out_specs=[pl.BlockSpec(memory_space=out_space) for _ in out_shape]
        if many
        else pl.BlockSpec(memory_space=out_space),
        scratch_shapes=list(scratch),
        compiler_params=pltpu.CompilerParams(vmem_limit_bytes=VMEM_LIMIT),
        cost_estimate=pl.CostEstimate(flops=flops, bytes_accessed=nbytes, transcendentals=0),
    )


def iota(shape, dim):
    return lax.broadcasted_iota(I32, shape, dim)


def pack_cotangent(cot_ref, out_ref):
    for peer in range(out_ref.shape[0]):
        block = cot_ref[:, 192 * peer : 192 * peer + 192]
        place = GRADS_ORDER.index(peer)
        out_ref[place, 0:128, :] = block[:, 0:128]
        out_ref[place, 128:192, :] = jnp.concatenate(
            [block[0:64, 128:192], block[64:128, 128:192]], axis=1
        )


def unpack_tokens(in_ref, out_ref, rows, sems):
    copies = []
    for pair in range(in_ref.shape[0] // 2):
        for peer in (2 * pair, 2 * pair + 1):
            place = ROWS_ORDER.index(peer)
            tail = in_ref[place, 128:192, :]
            rows[:, 192 * peer : 192 * peer + 128] = in_ref[place, 0:128, :]
            rows[:, 192 * peer + 128 : 192 * peer + 192] = jnp.concatenate(
                [tail[:, 0:64], tail[:, 64:128]], axis=0
            )
        columns = pl.ds(384 * pair, 384)
        copies.append(
            pltpu.make_async_copy(rows.at[:, columns], out_ref.at[:, columns], sems.at[pair])
        )
        copies[-1].start()
    for copy in copies:
        copy.wait()


def columns_of(row):
    return jnp.transpose(jnp.broadcast_to(row, (128, 128)))


def number_slots(me_ref, ids_ref, slot_ref, want_ref, id_cols, first_cols, first_rows):
    blocks = ids_ref.shape[0]
    me = me_ref[0] & 15
    ids = ids_ref[...].astype(F32)
    for i in range(blocks):
        id_cols[i] = columns_of(ids[i : i + 1, :])
    earlier = iota((128, 128), 0) < iota((128, 128), 1)
    for j in range(blocks):
        row = ids[j : j + 1, :]
        seen = jnp.where((id_cols[j] == row) & earlier, 1.0, 0.0)
        for i in range(j):
            seen = jnp.where(id_cols[i] == row, 1.0, seen)
        again = jnp.max(seen, axis=0, keepdims=True) > 0.0
        firsts = jnp.where(again, -1.0, row)
        first_rows[j : j + 1, :] = firsts
        first_cols[j] = columns_of(firsts)
    owner = jnp.floor((ids + 0.5) * (1.0 / VOCAB_ROWS))
    base = owner * float(VOCAB_ROWS)
    local_row = ids - base
    total_hi = jnp.zeros((8, 128), F32)
    total_lo = jnp.zeros((8, 128), F32)
    for j in range(blocks):
        row = ids[j : j + 1, :]
        low = base[j : j + 1, :]
        count = jnp.zeros((128, 128), F32)
        for i in range(blocks):
            other = first_cols[i]
            count = jnp.where((other >= low) & (other < row), count + 1.0, count)
        rank = jnp.sum(count, axis=0, keepdims=True).astype(I32)
        owner_j = owner[j : j + 1, :].astype(I32)
        slot_ref[j : j + 1, :] = (owner_j ^ FLIP) * CAP + rank
        relative = (owner_j ^ me) * CAP + rank
        is_first = first_rows[j : j + 1, :] >= 0.0
        local_j = local_row[j : j + 1, :].astype(I32)
        high = jnp.where(is_first, local_j >> 4, 0).astype(F32)
        lows = jnp.where(is_first, (local_j & 15) + 1, 0).astype(F32)
        left = jnp.where((relative >> 7) == iota((8, 128), 0), 1.0, 0.0).astype(BF16)
        here = (relative & 127) == iota((128, 128), 0)
        nt = (((1,), (1,)), ((), ()))
        total_hi += lax.dot_general(
            left, jnp.where(here, high, 0.0).astype(BF16), nt, preferred_element_type=F32
        )
        total_lo += lax.dot_general(
            left, jnp.where(here, lows, 0.0).astype(BF16), nt, preferred_element_type=F32
        )
    want = (total_hi * 16.0 + total_lo).astype(I32) - 1
    for x in range(4):
        want_ref[x] = want[2 * x : 2 * x + 2, :]


def wanted_rows(me, want):
    slots = 8 * 128
    position = iota((slots, 128), 0) ^ (((me & 15) ^ FLIP) * CAP)
    want_f = want.astype(F32)
    spread = jnp.zeros((slots, 128), F32)
    for r in range(8):
        spread = jnp.where((position >> 7) == r, want_f[r // 2, r % 2 : r % 2 + 1, :], spread)
    mine = jnp.where((position & 127) == iota((slots, 128), 1), spread, 0.0)
    return jnp.sum(mine, axis=1, keepdims=True).astype(I32)


def fetch_rows(me_ref, want_ref, table_ref, rows_ref):
    wanted = wanted_rows(me_ref[0], want_ref[...])
    slots, owned = wanted.shape[0], table_ref.shape[1]
    pick = jnp.where(wanted == iota((slots, owned), 1), 1.0, 0.0).astype(BF16)
    rows_ref[...] = lax.dot_general(
        pick, table_ref[...], (((1,), (1,)), ((), ())), preferred_element_type=F32
    ).astype(BF16)


def sum_slots(cols_ref, slot_ref, rows_ref, out_ref, columns):
    blocks = cols_ref.shape[0]
    slots = rows_ref.shape[0]
    for u in range(blocks):
        place = GRADS_ORDER.index(u)
        tail = cols_ref[place, 128:192, :]
        columns[128 * u : 128 * u + 128, 0:128] = cols_ref[place, 0:128, :]
        columns[128 * u : 128 * u + 128, 128:192] = jnp.concatenate(
            [tail[:, 0:64], tail[:, 64:128]], axis=0
        )
    member = jnp.concatenate(
        [
            jnp.where(slot_ref[u : u + 1, :] == iota((slots, 128), 0), 1.0, 0.0).astype(BF16)
            for u in range(blocks)
        ],
        axis=1,
    )
    grads = jnp.dot(member, columns[...], preferred_element_type=F32).astype(BF16)
    owners = slots // CAP
    rows = rows_ref[...]
    out_ref[:, 0:16, :] = rows[:, 0:128].reshape(owners, CAP, 128)
    out_ref[:, 16:32, :] = grads[:, 0:128].reshape(owners, CAP, 128)
    out_ref[:, 32:48, :] = jnp.concatenate([rows[:, 128:192], grads[:, 128:192]], axis=1).reshape(
        owners, CAP, 128
    )


def spread_tokens(got_ref, slot_ref, out_ref, ready, sems):
    blocks = slot_ref.shape[0]
    owners = got_ref.shape[0]
    slots = owners * CAP
    normalizer = math.sqrt(D)
    main = got_ref[:, 0:16, :].reshape(slots, 128)
    tail = got_ref[:, 32:48, :].reshape(slots, 128)[:, 0:64]
    rows = jnp.concatenate([main, tail], axis=1)
    slot_f = slot_ref[...].astype(F32)
    copies = []
    for u in range(blocks):
        mine = columns_of(slot_f[u : u + 1, :])
        pick = jnp.concatenate(
            [
                jnp.where(mine == (iota((128, 128), 1) + 128 * k).astype(F32), 1.0, 0.0).astype(BF16)
                for k in range(slots // 128)
            ],
            axis=1,
        )
        tokens = (jnp.dot(pick, rows, preferred_element_type=F32) * normalizer).astype(BF16)
        place = ROWS_ORDER.index(u)
        ready[place, 0:128, :] = tokens[:, 0:128]
        ready[place, 128:192, :] = jnp.concatenate(
            [tokens[0:64, 128:192], tokens[64:128, 128:192]], axis=1
        )
        copies.append(pltpu.make_async_copy(ready.at[place], out_ref.at[place], sems.at[u]))
        copies[-1].start()
    for copy in copies:
        copy.wait()


def update_rows(me_ref, want_ref, got_ref, table_ref, moment_ref, new_table_ref, new_moment_ref):
    normalizer = math.sqrt(D)
    wanted = wanted_rows(me_ref[0], want_ref[...])
    slots, owned = wanted.shape[0], table_ref.shape[1]
    pick = jnp.where(wanted == iota((slots, owned), 1), 1.0, 0.0).astype(BF16)
    main = got_ref[:, 16:32, :].reshape(slots, 128)
    tail = got_ref[:, 32:48, :].reshape(slots, 128)
    tn = (((0,), (0,)), ((), ()))
    ones = jnp.ones((8, slots), BF16)
    hits = jnp.dot(ones, pick, preferred_element_type=F32)
    touched = hits[0:1, :] > 0.0
    sum_main = lax.dot_general(main, pick, tn, preferred_element_type=F32)
    sum_tail = lax.dot_general(tail, pick, tn, preferred_element_type=F32)[64:128, :]
    for lo, hi, summed in ((0, 128, sum_main), (128, 192, sum_tail)):
        gradient = summed * normalizer
        old_table = table_ref[lo:hi, :]
        old_moment = moment_ref[lo:hi, :]
        weights = old_table.astype(F32)
        moment_new = beta_two * old_moment.astype(F32) + (1.0 - beta_two) * gradient * gradient
        denominator = jnp.sqrt(moment_new / (1.0 - beta_two**STEP)) + epsilon
        updated = weights - learn_rate * (gradient / denominator + weight_decay * weights)
        new_table_ref[lo:hi, :] = jnp.where(touched, updated, weights).astype(BF16)
        new_moment_ref[lo:hi, :] = jnp.where(
            touched, moment_new, old_moment.astype(F32)
        ).astype(BF16)


def exchange_requests(want, dp_count):
    across_x = [[x * 16 + rest for x in range(4)] for rest in range(16)]
    want = lax.all_to_all(
        want, "dp", split_axis=0, concat_axis=0, tiled=True, axis_index_groups=across_x
    )
    position = iota(want.shape, 1) * 8 + iota(want.shape, 2) // CAP
    for bit in (1, 2, 4, 8):
        got = lax.ppermute(want, "dp", [(g, g ^ bit) for g in range(dp_count)])
        want = jnp.where((position & bit) != 0, got, want)
    return want


def local(token_ids, embed_table, second_moment, cotangent):
    dp_count = lax.axis_size("dp")
    seq_count = lax.axis_size("seq")
    blocks = token_ids.shape[0] // 128
    slots = dp_count * CAP
    owned = embed_table.shape[0]
    S = jax.ShapeDtypeStruct
    me = lax.axis_index("dp").astype(I32).reshape(1)
    table = embed_table.T
    moment = second_moment.T
    ids = token_ids.reshape(blocks, 128)

    packed = call(pack_cotangent, S((seq_count, 192, 128), BF16), 1, nbytes=1200000)(cotangent)
    columns = lax.all_to_all(
        packed, "seq", split_axis=0, concat_axis=0, tiled=True, axis_index_groups=[GRADS_ORDER]
    )
    slot, want = call(
        number_slots,
        (S((blocks, 128), I32), S((4, 2, 128), I32)),
        2,
        scratch=[
            pltpu.VMEM((blocks, 128, 128), F32),
            pltpu.VMEM((blocks, 128, 128), F32),
            pltpu.VMEM((16, 128), F32),
        ],
        smem_in=(0,),
        flops=10**6,
        nbytes=10**6,
    )(me, ids)
    want = exchange_requests(want, dp_count)
    rows = call(
        fetch_rows, S((slots, 192), BF16), 3, smem_in=(0,), flops=2 * slots * owned * 192, nbytes=1200000
    )(me, want, table)
    payload = call(
        sum_slots,
        S((dp_count, 48, 128), BF16),
        3,
        scratch=[pltpu.VMEM((blocks * 128, 192), BF16)],
        flops=2 * slots * blocks * 128 * 192,
        nbytes=1800000,
    )(columns, slot, rows)
    flipped = [[k ^ FLIP for k in range(dp_count)]]
    got = lax.all_to_all(
        payload, "dp", split_axis=0, concat_axis=0, tiled=True, axis_index_groups=flipped
    )
    tokens = call(
        spread_tokens,
        S((seq_count, 192, 128), BF16),
        2,
        scratch=[pltpu.VMEM((seq_count, 192, 128), BF16), pltpu.SemaphoreType.DMA((blocks,))],
        out_space=pl.ANY,
        flops=2 * slots * blocks * 128 * 192,
        nbytes=1400000,
    )(got, slot)
    arrived = lax.all_to_all(
        tokens, "seq", split_axis=0, concat_axis=0, tiled=True, axis_index_groups=[ROWS_ORDER]
    )
    new_table, new_moment = call(
        update_rows,
        (S((192, owned), BF16), S((192, owned), BF16)),
        5,
        smem_in=(0,),
        flops=2 * slots * owned * 192,
        nbytes=4000000,
    )(me, want, got, table, moment)
    embedded = call(
        unpack_tokens,
        S((128, seq_count * 192), BF16),
        1,
        scratch=[
            pltpu.VMEM((128, seq_count * 192), BF16),
            pltpu.SemaphoreType.DMA((seq_count // 2,)),
        ],
        out_space=pl.ANY,
        nbytes=1200000,
    )(arrived)
    return embedded, new_table.T, new_moment.T


def solution(mesh):
    in_specs = (P("dp"), P("dp", "seq"), P("dp", "seq"), P(("dp", "seq"), None))
    out_specs = (P(("dp", "seq"), None), P("dp", "seq"), P("dp", "seq"))
    return jax.shard_map(local, mesh=mesh, in_specs=in_specs, out_specs=out_specs, check_vma=False)
```
